32 devices in a mesh: grp: 4 (over z), rve: 8 (over y, x, core).
Axes of the slice: x: 2, y: 2, z: 4, core: 2. Of those that a mesh axis runs over, the one named last changes fastest.
Arguments:
- displacement: float32 [3, 64, 32, 128], P(None, ('grp', 'rve')), may hold values from -6 to 6
- stiffness: bfloat16 [27, 3, 3, 64, 32, 128], P(None, None, None, ('grp', 'rve')), may hold values from -0.65625 to 0.65625
- external: float32 [3, 64, 32, 128], P(None, ('grp', 'rve')), may hold values from -6 to 6
- point_node: int32 [8], P('grp'), may hold values from 0 to 65535
- point_owner: int32 [8, 1], P('grp'), may hold values from 0 to 3; in each aligned block of 2 rows (0 to 1, 2 to 3, ...) no two rows name the same one
- point_load: float32 [8, 18], P('grp'), may hold values from -6 to 6
- moduli_diag: float32 [4, 6, 8, 64, 128], P('grp', None, 'rve'), may hold values from 1.5 to 4
- moduli_off: float32 [4, 36, 8, 64, 128], P('grp', None, 'rve'), may hold values from -1 to 1
- schmid: float32 [4, 72, 8, 64, 128], P('grp', None, 'rve'), may hold values from -1 to 1
- crss: float32 [4, 12, 8, 64, 128], P('grp', None, 'rve'), may hold values from 0.3 to 3
- branch: int32 [4, 8, 64, 128], P('grp', 'rve'), may hold values from 0 to 4095
- rate: float32 [4, 8, 64, 128], P('grp', 'rve'), may hold values from 0.03 to 0.3
Outputs:
- residual: float32 [3, 64, 32, 128], P(None, ('grp', 'rve'))
- point_stress: float32 [8, 6], P('grp')
The draws below stay inside these ranges and needn't reach their ends.
Inputs may be any that keep to these rules, and one draw needn't show every extreme that they name: `point_owner`: among the 2 points of one quarter's list, at most 1 name the same volume, a bound that some block reaches.
All inputs are finite; a program needn't handle non-finite values.
Results may differ from the reference program's by a relative error of at most 0.0003.
Values sent between devices are 32-bit elements; how exact they have to be, the bound alone decides.
A program may use at most 128 MiB of HBM per device.

```python
import math
import jax
import jax.numpy as jnp
import numpy as np
from jax import lax

XD = 2
NY = 32
NZ = 128
P_Q = 2
VY = 64
VZ = 128
SLIP = 12
SWEEPS = 10
CAP = 1
NX = 64
P_TOTAL = 8
VOX = 8
N_GRP = 4
N_RVE = 8


def set_ends(entries, own_key, smallest, top_value):
    place = [jax.random.randint(jax.random.fold_in(own_key, axis), (), 0, length) for axis, length in enumerate(entries.shape)]
    longest = entries.shape.index(max(entries.shape))
    neighbour = place[:longest] + [(place[longest] + 1) % entries.shape[longest]] + place[longest + 1:]
    return entries.at[tuple(place)].set(smallest).at[tuple(neighbour)].set(top_value)


def levels(key, shape, pieces, smallest, top_value):
    gain = 1.0
    for axis_at, shards_of in pieces:
        draws = jax.random.uniform(jax.random.fold_in(jax.random.fold_in(key, 6), axis_at), (shards_of,), jnp.float32, smallest / len(pieces), top_value / len(pieces))
        gain = gain * jnp.repeat(jnp.exp(draws), shape[axis_at] // shards_of).reshape((-1,) + (1,) * (len(shape) - 1 - axis_at))
    return gain


def routed_block(key, own, number, rows, number_of, top, limit, lean):
    ranking = jax.random.permutation(key, number_of)
    crowded, usual = shares(number_of, rows * top, limit, lean, True), shares(number_of, rows * top, limit, lean, False)
    places = jnp.arange(number_of)

    def named(sizes, rotation):
        used = int((sizes > 0).sum())
        fixed = max(1, used // 4)
        passed = fixed + (places - fixed + rotation * (used - fixed)) % max(1, number_of - fixed)
        return jnp.zeros((number_of,), jnp.int32).at[ranking[jnp.where(places < fixed, places, passed)]].set(jnp.asarray(sizes, jnp.int32))

    sizes = jnp.where(number % 4 == 0, named(crowded, number // 4), named(usual, number - number // 4 - 1))
    mixed = jax.random.permutation(jax.random.fold_in(own, 3), number_of)
    donor, sink = mixed[0:number_of // 2 * 2:2], mixed[1:number_of // 2 * 2:2]
    room = jnp.minimum(sizes[donor] - 1, limit - sizes[sink]) // 2
    room = jnp.where((donor == ranking[0]) | (sink == ranking[0]) | (sizes[sink] == 0), 0, jnp.maximum(room, 0))
    passed = jax.random.randint(jax.random.fold_in(own, 4), (number_of // 2,), 0, 1 << 20) % (room + 1)
    sizes = sizes.at[donor].add(-passed).at[sink].add(passed)
    items = jnp.searchsorted(jnp.cumsum(sizes), jnp.arange(rows * top), side="right").astype(jnp.int32)
    table = items.reshape(top, rows).T
    table = table[jax.random.permutation(jax.random.fold_in(own, 1), rows)]
    rotation = jax.random.randint(jax.random.fold_in(own, 2), (rows, 1), 0, top)
    return jnp.take_along_axis(table, (jnp.arange(top)[None, :] + rotation) % top, axis=1)


def shares(number_of, total, most, lean, full):
    weights = [(1 << 20) // math.isqrt(grade ** lean) + 1 for grade in range(1, number_of + 1)]
    largest = most if full else min(most, max(-(-total // number_of), total * weights[0] // sum(weights)))
    least = 1 if total - largest >= number_of - 1 else 0
    given, rest = [largest] + [least] * (number_of - 1), total - largest - least * (number_of - 1)
    while rest > 0:
        free = [i for i in range(1, number_of) if given[i] < largest] or [i for i in range(1, number_of) if given[i] < most]
        pool, left = sum([weights[i] for i in free]), rest
        for i in free:
            more = min(most - given[i], max(1, left * weights[i] // pool), rest)
            given[i] = given[i] + more
            rest = rest - more
    return np.array(given)


def scatter_about(own_key, shape, scale, limit, cuts=(), held_as=jnp.bfloat16):
    entries = jax.random.normal(own_key, shape, jnp.float32) * scale
    if len(cuts) > 0:
        entries = levels(own_key, shape, cuts, -0.22, 0.18) * entries
    return jnp.clip(entries, min=-limit, max=limit).astype(held_as)


def setup_inputs(seed: int = 0) -> dict:
    seeds = jax.random.split(jax.random.key(seed), 13)
    displacement = scatter_about(seeds[0], (3, NX, NY, NZ), 1.0, 6.0, ((1, 32),), jnp.float32)
    stiffness = scatter_about(seeds[1], (27, 3, 3, NX, NY, NZ), 0.11, 0.65625, ((3, 32),))
    external = scatter_about(seeds[2], (3, NX, NY, NZ), 1.0, 6.0, ((1, 32),), jnp.float32)
    point_node = set_ends(jax.random.randint(seeds[3], (P_TOTAL,), 0, XD * N_RVE * NY * NZ), jax.random.fold_in(seeds[3], 1), 0, (XD * N_RVE * NY * NZ) - 1).astype(jnp.int32)
    point_owner_keys = jax.random.split(jax.random.fold_in(seeds[4], 1), P_TOTAL // P_Q)
    point_owner_turns = jax.random.permutation(jax.random.fold_in(seeds[4], 3), P_TOTAL // P_Q)
    point_owner = jax.vmap(lambda own, number: routed_block(jax.random.fold_in(seeds[4], 2), own, number, P_Q, N_GRP, 1, CAP, 2))(point_owner_keys, point_owner_turns).reshape((P_TOTAL, 1))
    point_load = scatter_about(seeds[5], (P_TOTAL, 18), 1 ** -0.5, 6.0, ((0, 4),), jnp.float32)
    moduli_diag = jnp.clip(jnp.exp(math.log(4.0) - 0.98082925 * jax.random.uniform(seeds[6], (N_GRP, 6, VOX, VY, VZ), jnp.float32) ** levels(seeds[6], (N_GRP, 6, VOX, VY, VZ), ((0, 4), (2, 8)), -0.2, 0.2)), 1.5, 4.0)
    moduli_off = scatter_about(seeds[7], (N_GRP, 36, VOX, VY, VZ), 0.2, 1.0, ((0, 4), (2, 8)), jnp.float32)
    schmid = scatter_about(seeds[8], (N_GRP, 72, VOX, VY, VZ), 0.25, 1.0, ((0, 4), (2, 8)), jnp.float32)
    crss = jnp.clip(jnp.exp(math.log(3.0) - 2.3025851 * jax.random.uniform(seeds[9], (N_GRP, 12, VOX, VY, VZ), jnp.float32) ** levels(seeds[9], (N_GRP, 12, VOX, VY, VZ), ((0, 4), (2, 8)), -0.2, 0.2)), 0.3, 3.0)
    branch = set_ends(jax.random.randint(seeds[10], (N_GRP, VOX, VY, VZ), 0, 4096), jax.random.fold_in(seeds[10], 1), 0, 4095).astype(jnp.int32)
    rate = jnp.clip(jnp.exp(math.log(0.3) - 2.3025852 * jax.random.uniform(seeds[11], (N_GRP, VOX, VY, VZ), jnp.float32) ** levels(seeds[11], (N_GRP, VOX, VY, VZ), ((0, 4), (1, 8)), -0.2, 0.2)), 0.03, 0.3)
    return dict(displacement=displacement, stiffness=stiffness, external=external, point_node=point_node, point_owner=point_owner, point_load=point_load, moduli_diag=moduli_diag, moduli_off=moduli_off, schmid=schmid, crss=crss, branch=branch, rate=rate)


RELAX = 0.15
NEIGHBOUR_WEIGHT = 1.0 / 6.0


def stiff_apply(blocks, padded):
    extent = (padded.shape[1] - 2, padded.shape[2] - 2, padded.shape[3] - 2)
    summed = jnp.zeros((3,) + extent, jnp.float32)
    for i in range(3):
        for j in range(3):
            for k in range(3):
                offset = i * 9 + j * 3 + k
                window = padded[:, i:i + extent[0], j:j + extent[1], k:k + extent[2]]
                summed = summed + jnp.sum(blocks[offset].astype(jnp.float32) * window[None], axis=1)
    return summed


def node_strain(padded):
    extent = (padded.shape[1] - 2, padded.shape[2] - 2, padded.shape[3] - 2)

    def gradient(c, k):
        lower = [slice(1, 1 + extent[0]), slice(1, 1 + extent[1]), slice(1, 1 + extent[2])]
        upper = list(lower)
        lower[k] = slice(0, extent[k])
        upper[k] = slice(2, 2 + extent[k])
        return (padded[c][tuple(upper)] - padded[c][tuple(lower)]) * 0.5

    table = [[gradient(c, k) for k in range(3)] for c in range(3)]
    return jnp.stack([table[0][0], table[1][1], table[2][2], table[1][2] + table[2][1],
                      table[0][2] + table[2][0], table[0][1] + table[1][0]])


def activity(branch):
    bit_index = jnp.arange(SLIP, dtype=jnp.int32)
    return (jnp.right_shift(branch[None], bit_index[:, None, None, None]) & 1).astype(jnp.float32)


def make_entry(diagonal, offdiag, schmid_rows, critical, plastic_rate):
    matrix = offdiag.reshape((6, 6) + offdiag.shape[1:]) + jnp.eye(6, dtype=jnp.float32)[:, :, None, None, None] * diagonal[None]
    schmid_mat = schmid_rows.reshape((12, 6) + schmid_rows.shape[1:])
    return (matrix, schmid_mat, critical[:, None], plastic_rate[:, None], jnp.swapaxes(schmid_mat, 0, 1))


def contract(matrix, field):
    summed = matrix[:, 0][:, None] * field[0][None]
    for j in range(1, matrix.shape[1]):
        summed = summed + matrix[:, j][:, None] * field[j][None]
    return summed


def sweeps(ebar, entry, plane_sum):
    baseline = ebar[:, :, None, None, None]
    matrix, schmid_mat, critical, plastic_rate, schmid_back = entry
    shape = (6, ebar.shape[1]) + matrix.shape[2:]
    fluctuation = jnp.zeros(shape, jnp.float32)
    plastic = jnp.zeros(shape, jnp.float32)
    for sweep in range(SWEEPS):
        strain = baseline + fluctuation - plastic
        stress = contract(matrix, strain)
        resolved = contract(schmid_mat, stress)
        slipped = plastic_rate * (resolved - critical * jnp.tanh(resolved / critical))
        plastic = plastic + contract(schmid_back, slipped)
        beside = plane_sum(strain, stress) + jnp.roll(stress, 1, axis=3) + jnp.roll(stress, -1, axis=3)
        beside = beside + jnp.roll(stress, 1, axis=4) + jnp.roll(stress, -1, axis=4)
        fluctuation = fluctuation - RELAX * (stress - NEIGHBOUR_WEIGHT * beside)
    final_strain = baseline + fluctuation - plastic
    return contract(matrix, final_strain)


def roll_planes(strain, stress):
    return jnp.roll(stress, 1, axis=2) + jnp.roll(stress, -1, axis=2)


def reference(displacement, stiffness, external, point_node, point_owner, point_load, moduli_diag, moduli_off, schmid, crss, branch, rate):
    padded = jnp.pad(displacement, ((0, 0), (1, 1), (1, 1), (1, 1)))
    applied = stiff_apply(stiffness, padded)
    strain_field = node_strain(padded).reshape(6, -1)
    quarter_of = (jnp.arange(P_TOTAL, dtype=jnp.int32) // P_Q).astype(jnp.int32)
    flat_node = (quarter_of * (XD * N_RVE * NY * NZ) + point_node).astype(jnp.int32)
    ebar = strain_field[:, flat_node].T

    def one_point(inputs):
        strain_point, owner_id = inputs
        plastic_rate = activity(branch[owner_id]) * rate[owner_id]
        entry = make_entry(moduli_diag[owner_id], moduli_off[owner_id], schmid[owner_id], crss[owner_id], plastic_rate)
        final = sweeps(strain_point[:, None], entry, roll_planes)
        return jnp.sum(final, axis=(1, 2, 3, 4)) / (VOX * VY * VZ)

    point_stress = lax.map(one_point, (ebar, point_owner[:, 0]))
    force = jnp.einsum("pcj,pj->pc", point_load.reshape(-1, 3, 6), point_stress, precision=lax.Precision.HIGHEST)
    flat = (external - applied).reshape(3, -1).at[:, flat_node].add(-force.T)
    return flat.reshape(external.shape), point_stress
```

```python
import functools
import jax
import jax.numpy as jnp
from jax import lax
from jax.experimental import pallas as pl
from jax.experimental.pallas import tpu as pltpu
from jax.sharding import PartitionSpec as P

MESH = pl.DeviceIdType.MESH

SLIP = 12
SWEEPS = 10


RELAX = 0.15
NEIGHBOUR_WEIGHT = 1.0 / 6.0


def padded_2(value, sides, width, wrap):
    for axis, dim in sides:
        count, length = (lax.axis_size(axis), value.shape[dim])
        up = [(i, (i + 1) % count) for i in range(count if wrap else count - 1)]
        down = [(j, i) for i, j in up]
        last = lax.slice_in_dim(value, length - width, length, axis=dim)
        first = lax.slice_in_dim(value, 0, width, axis=dim)
        before = lax.ppermute(last, axis, up)
        after = lax.ppermute(first, axis, down)
        value = jnp.concatenate([before, value, after], axis=dim)
    return value


def stiff_apply(blocks, padded):
    extent = (padded.shape[1] - 2, padded.shape[2] - 2, padded.shape[3] - 2)
    summed = jnp.zeros((3,) + extent, jnp.float32)
    for i in range(3):
        for j in range(3):
            for k in range(3):
                offset = i * 9 + j * 3 + k
                window = padded[:, i : i + extent[0], j : j + extent[1], k : k + extent[2]]
                summed = summed + jnp.sum(blocks[offset].astype(jnp.float32) * window[None], axis=1)
    return summed


def node_strain(padded):
    extent = (padded.shape[1] - 2, padded.shape[2] - 2, padded.shape[3] - 2)

    def gradient(c, k):
        lower = [slice(1, 1 + extent[0]), slice(1, 1 + extent[1]), slice(1, 1 + extent[2])]
        upper = list(lower)
        lower[k] = slice(0, extent[k])
        upper[k] = slice(2, 2 + extent[k])
        return (padded[c][tuple(upper)] - padded[c][tuple(lower)]) * 0.5

    table = [[gradient(c, k) for k in range(3)] for c in range(3)]
    return jnp.stack(
        [
            table[0][0],
            table[1][1],
            table[2][2],
            table[1][2] + table[2][1],
            table[0][2] + table[2][0],
            table[0][1] + table[1][0],
        ]
    )


def activity(branch):
    bit_index = jnp.arange(SLIP, dtype=jnp.int32)
    return (jnp.right_shift(branch[None], bit_index[:, None, None, None]) & 1).astype(jnp.float32)


def elastic_matrix(diagonal, offdiag):
    return (
        offdiag.reshape((6, 6) + offdiag.shape[1:])
        + jnp.eye(6, dtype=jnp.float32)[:, :, None, None, None] * diagonal[None]
    )


def make_entry(diagonal, offdiag, schmid_rows, critical, plastic_rate):
    matrix = elastic_matrix(diagonal, offdiag)
    schmid_mat = schmid_rows.reshape((12, 6) + schmid_rows.shape[1:])
    return (
        matrix,
        schmid_mat,
        critical[:, None],
        plastic_rate[:, None],
        jnp.swapaxes(schmid_mat, 0, 1),
    )


def contract(matrix, field):
    summed = matrix[:, 0][:, None] * field[0][None]
    for j in range(1, matrix.shape[1]):
        summed = summed + matrix[:, j][:, None] * field[j][None]
    return summed


def sweeps(ebar, entry, plane_sum):
    baseline = ebar[:, :, None, None, None]
    matrix, schmid_mat, critical, plastic_rate, schmid_back = entry
    shape = (6, ebar.shape[1]) + matrix.shape[2:]
    fluctuation = jnp.zeros(shape, jnp.float32)
    plastic = jnp.zeros(shape, jnp.float32)
    for sweep in range(SWEEPS):
        strain = baseline + fluctuation - plastic
        stress = contract(matrix, strain)
        resolved = contract(schmid_mat, stress)
        slipped = plastic_rate * (resolved - critical * jnp.tanh(resolved / critical))
        plastic = plastic + contract(schmid_back, slipped)
        beside = (
            plane_sum(strain, stress) + jnp.roll(stress, 1, axis=3) + jnp.roll(stress, -1, axis=3)
        )
        beside = beside + jnp.roll(stress, 1, axis=4) + jnp.roll(stress, -1, axis=4)
        fluctuation = fluctuation - RELAX * (stress - NEIGHBOUR_WEIGHT * beside)
    final_strain = baseline + fluctuation - plastic
    return contract(matrix, final_strain)


def ring_place(index):
    high, low = index // 4, index % 4
    return 4 * high + 2 * ((low // 2 + high) % 2) + low % 2


def volume_kernel(
    members,
    ebar,
    diag,
    off,
    schmid,
    crss,
    branch,
    rate,
    out,
    diag_v,
    off_v,
    schmid_v,
    crss_v,
    branch_v,
    rate_v,
    strain_v,
    stress_v,
    edge_v,
    halo_v,
    send_sems,
    recv_sems,
    local_sems,
    edge_send,
    edge_recv,
):
    me = lax.axis_index("rve")
    place = ring_place(me)
    sources = [off, diag, schmid, crss, branch, rate]
    targets = [off_v, diag_v, schmid_v, crss_v, branch_v, rate_v]
    barrier = pltpu.get_barrier_semaphore()
    for k in range(1, members):
        pl.semaphore_signal(
            barrier, inc=1, device_id={"rve": (me + k) % members}, device_id_type=MESH
        )
    pl.semaphore_wait(barrier, members - 1)

    def block_of(source, device):
        rows = pl.ds(pl.multiple_of(ring_place(device) * 8, 8), 8)
        return source.at[0, :, 0, rows, :]

    copies = []
    for n in range(6):
        for k in range(1, members):
            peer = (me + k) % members
            copy = pltpu.make_async_remote_copy(
                src_ref=block_of(sources[n], peer),
                dst_ref=targets[n].at[me],
                send_sem=send_sems.at[n, k],
                recv_sem=recv_sems.at[n, k],
                device_id={"rve": peer},
                device_id_type=MESH,
            )
            copy.start()
            copies.append(copy)
        local = pltpu.make_async_copy(
            block_of(sources[n], me), targets[n].at[me], local_sems.at[n]
        )
        local.start()
        copies.append(local)
    for copy in copies:
        copy.wait()

    def prepare(v, carry):
        for i in range(6):
            off_v[v, 7 * i] = off_v[v, 7 * i] + diag_v[v, i]
        bits, speed = branch_v[v, 0], rate_v[v, 0]
        for a in range(SLIP):
            critical = crss_v[v, a]
            inverse = 1.0 / critical
            for i in range(6):
                schmid_v[v, 6 * a + i] = schmid_v[v, 6 * a + i] * inverse
            active = ((bits >> a) & 1).astype(jnp.float32)
            crss_v[v, a] = active * speed * (critical * critical)
        for p in range(points):
            for i in range(6):
                strain_v[v, 6 * p + i] = jnp.full((8, 128), ebar[p, i], jnp.float32)
        return carry

    points = ebar.shape[0]
    parts = 6 * points
    lax.fori_loop(0, members, prepare, 0)

    def elastic(v, strain):
        stress = []
        for i in range(6):
            sums = [None] * points
            for j in range(6):
                c = off_v[v, 6 * i + j]
                for p in range(points):
                    term = c * strain[6 * p + j]
                    sums[p] = term if j == 0 else sums[p] + term
            stress.append(sums)
        return [stress[i][p] for p in range(points) for i in range(6)]

    def keep(v, now, stress):
        for k in range(parts):
            stress_v[now, v, k] = stress[k]
            edge_v[now, 0, v, k : k + 1, :] = stress[k][7:8, :]
            edge_v[now, 1, v, k : k + 1, :] = stress[k][0:1, :]

    def first(v, carry):
        keep(v, 0, elastic(v, [strain_v[v, k] for k in range(parts)]))
        return carry

    lax.fori_loop(0, members, first, 0)
    following = ring_place((place + 1) % members)
    previous = ring_place((place + members - 1) % members)
    row = lax.broadcasted_iota(jnp.int32, (8, 128), 0)
    top, bottom = row == 0, row == 7

    def edge_copy(now, way):
        return pltpu.make_async_remote_copy(
            src_ref=edge_v.at[now, way],
            dst_ref=halo_v.at[now, way],
            send_sem=edge_send.at[now, way],
            recv_sem=edge_recv.at[now, way],
            device_id={"rve": following if way == 0 else previous},
            device_id_type=MESH,
        )

    def slip(now, v):
        for half in range(0, points, 2):
            pair = range(half, min(half + 2, points))
            stress = {(p, i): stress_v[now, v, 6 * p + i] for p in pair for i in range(6)}
            change = {}
            for a in range(SLIP):
                rows = [schmid_v[v, 6 * a + i] for i in range(6)]
                weight = crss_v[v, a]
                for p in pair:
                    ratio = rows[0] * stress[p, 0]
                    for i in range(1, 6):
                        ratio = ratio + rows[i] * stress[p, i]
                    slipped = weight * (ratio - jnp.tanh(ratio))
                    for i in range(6):
                        term = rows[i] * slipped
                        change[p, i] = term if a == 0 else change[p, i] + term
            for p in pair:
                for i in range(6):
                    strain_v[v, 6 * p + i] = strain_v[v, 6 * p + i] - change[p, i]

    def advance(now, v):
        before, after = (v + members - 1) % members, (v + 1) % members
        strain = []
        for k in range(parts):
            stress = stress_v[now, v, k]
            above = jnp.where(top, halo_v[now, 0, v, k : k + 1, :], pltpu.roll(stress, 1, 0))
            below = jnp.where(bottom, halo_v[now, 1, v, k : k + 1, :], pltpu.roll(stress, 7, 0))
            beside = (stress_v[now, before, k] + stress_v[now, after, k]) + (above + below)
            beside = beside + (pltpu.roll(stress, 1, 1) + pltpu.roll(stress, 127, 1))
            value = strain_v[v, k] - RELAX * (stress - NEIGHBOUR_WEIGHT * beside)
            strain_v[v, k] = value
            strain.append(value)
        keep(v, 1 - now, elastic(v, strain))

    def sweep(s, carry):
        now = s % 2
        edges = [edge_copy(now, way) for way in range(2)]
        for copy in edges:
            copy.start()

        def slip_plane(v, inner):
            slip(now, v)
            return inner

        def advance_plane(v, inner):
            advance(now, v)
            return inner

        lax.fori_loop(0, members, slip_plane, 0)
        for copy in edges:
            copy.wait()
        lax.fori_loop(0, members, advance_plane, 0)
        return carry

    lax.fori_loop(0, SWEEPS, sweep, 0)
    last = SWEEPS % 2
    for k in range(parts):
        total = stress_v[last, 0, k]
        for v in range(1, members):
            total = total + stress_v[last, v, k]
        out[k] = total


def volume_sums(ebar, diag, off, schmid, crss, branch, rate):
    members = lax.axis_size("rve")
    points = ebar.shape[0]
    any_space = pl.BlockSpec(memory_space=pl.ANY)

    def held(count, dtype=jnp.float32):
        return pltpu.VMEM((members, count, 8, 128), dtype)

    parts = 6 * points
    sums = pl.pallas_call(
        functools.partial(volume_kernel, members),
        out_shape=jax.ShapeDtypeStruct((parts, 8, 128), jnp.float32),
        in_specs=[pl.BlockSpec(memory_space=pltpu.SMEM)] + [any_space] * 6,
        out_specs=pl.BlockSpec(memory_space=pltpu.VMEM),
        scratch_shapes=[
            held(6),
            held(36),
            held(72),
            held(12),
            held(1, jnp.int32),
            held(1),
            held(parts),
            pltpu.VMEM((2, members, parts, 8, 128), jnp.float32),
            pltpu.VMEM((2, 2, members, parts, 128), jnp.float32),
            pltpu.VMEM((2, 2, members, parts, 128), jnp.float32),
            pltpu.SemaphoreType.DMA((6, members)),
            pltpu.SemaphoreType.DMA((6, members)),
            pltpu.SemaphoreType.DMA((6,)),
            pltpu.SemaphoreType.DMA((2, 2)),
            pltpu.SemaphoreType.DMA((2, 2)),
        ],
        compiler_params=pltpu.CompilerParams(
            collective_id=0, has_side_effects=True, vmem_limit_bytes=40 * 1024 * 1024
        ),
        cost_estimate=pl.CostEstimate(
            flops=20 * 180 * parts * members * 1024, bytes_accessed=8 << 20, transcendentals=0
        ),
    )(ebar, diag, off, schmid, crss, branch[None], rate[None])
    return jnp.sum(sums, axis=(1, 2))


def plane_sums(ebar, moduli_diag, moduli_off, schmid, crss, branch, rate):
    plastic_rate = activity(branch[0]) * rate[0]
    entry = make_entry(moduli_diag[0], moduli_off[0], schmid[0], crss[0], plastic_rate)

    def plane_sum(strain, stress):
        rimmed = padded_2(stress, (("rve", 2),), 1, True)
        return rimmed[:, :, :-2] + rimmed[:, :, 2:]

    final = sweeps(ebar, entry, plane_sum)
    return jnp.sum(final, axis=(2, 3, 4))


def per_device(
    displacement,
    stiffness,
    external,
    point_node,
    point_owner,
    point_load,
    moduli_diag,
    moduli_off,
    schmid,
    crss,
    branch,
    rate,
):
    extended = padded_2(displacement, ((("grp", "rve"), 1),), 1, False)
    padded = jnp.pad(extended, ((0, 0), (0, 0), (1, 1), (1, 1)))
    applied = stiff_apply(stiffness, padded)
    strain_field = node_strain(padded).reshape(6, -1)
    groups = lax.axis_size("grp")
    members = lax.axis_size("rve")
    member = lax.axis_index("rve")
    local_nodes = strain_field.shape[1]
    shifted_node = point_node - member * local_nodes
    present = ((shifted_node >= 0) & (shifted_node < local_nodes)).astype(jnp.float32)
    safe_node = jnp.clip(shifted_node, 0, local_nodes - 1)
    partial_value = strain_field[:, safe_node].T * present[:, None]
    count = point_owner.shape[0]
    capacity = count // 2
    owner = point_owner[:, 0]
    onehot = (owner[:, None] == jnp.arange(groups, dtype=jnp.int32)[None, :]).astype(jnp.float32)
    ranked = jnp.cumsum(onehot, axis=0) - onehot
    slot_of = jnp.sum(ranked * onehot, axis=1)
    slot_match = (
        slot_of[None, None, :] == jnp.arange(capacity, dtype=jnp.float32)[None, :, None]
    ).astype(jnp.float32)
    select = onehot.T[:, None, :] * slot_match
    quarter = lax.psum(partial_value, "rve")
    outgoing = jnp.einsum("gsp,pi->gsi", select, quarter, precision=lax.Precision.HIGHEST)
    arrived = lax.all_to_all(outgoing, "grp", split_axis=0, concat_axis=0, tiled=True)
    ebar = arrived.reshape(-1, 6).T
    voxels = members * rate.shape[1] * rate.shape[2] * rate.shape[3]
    if members == 8 and rate.shape[1:] == (1, 64, 128):
        local_sums = volume_sums(ebar.T, moduli_diag, moduli_off, schmid, crss, branch, rate)
        local_sums = local_sums.reshape(-1, 6).T
    else:
        local_sums = plane_sums(ebar, moduli_diag, moduli_off, schmid, crss, branch, rate)
    totals = lax.psum(local_sums, "rve") / voxels
    returned = lax.all_to_all(
        jnp.transpose(totals.reshape(6, groups, capacity), (1, 2, 0)),
        "grp",
        split_axis=0,
        concat_axis=0,
        tiled=True,
    )
    point_stress = jnp.einsum("gsp,gsi->pi", select, returned, precision=lax.Precision.HIGHEST)
    force = jnp.einsum(
        "pcj,pj->pc", point_load.reshape(-1, 3, 6), point_stress, precision=lax.Precision.HIGHEST
    )
    flat = (external - applied).reshape(3, -1).at[:, safe_node].add(-(force * present[:, None]).T)
    return (flat.reshape(external.shape), point_stress)


def solution(mesh):
    in_specs = (
        P(None, ("grp", "rve"), None, None),
        P(None, None, None, ("grp", "rve"), None, None),
        P(None, ("grp", "rve"), None, None),
        P("grp"),
        P("grp", None),
        P("grp", None),
        P("grp", None, "rve", None, None),
        P("grp", None, "rve", None, None),
        P("grp", None, "rve", None, None),
        P("grp", None, "rve", None, None),
        P("grp", "rve", None, None),
        P("grp", "rve", None, None),
    )
    out_specs = (P(None, ("grp", "rve"), None, None), P("grp", None))
    return jax.shard_map(
        per_device, mesh=mesh, in_specs=in_specs, out_specs=out_specs, check_vma=False
    )
```

```python
import functools
import jax
import jax.numpy as jnp
from jax import lax
from jax.experimental import pallas as pl
from jax.experimental.pallas import tpu as pltpu
from jax.sharding import PartitionSpec as P

MESH = pl.DeviceIdType.MESH
CHUNK = 2

SLIP = 12
SWEEPS = 10


RELAX = 0.15
NEIGHBOUR_WEIGHT = 1.0 / 6.0


def padded_2(value, sides, width, wrap):
    for axis, dim in sides:
        count, length = (lax.axis_size(axis), value.shape[dim])
        up = [(i, (i + 1) % count) for i in range(count if wrap else count - 1)]
        down = [(j, i) for i, j in up]
        last = lax.slice_in_dim(value, length - width, length, axis=dim)
        first = lax.slice_in_dim(value, 0, width, axis=dim)
        before = lax.ppermute(last, axis, up)
        after = lax.ppermute(first, axis, down)
        value = jnp.concatenate([before, value, after], axis=dim)
    return value


def stiff_apply(blocks, padded):
    extent = (padded.shape[1] - 2, padded.shape[2] - 2, padded.shape[3] - 2)
    summed = jnp.zeros((3,) + extent, jnp.float32)
    for i in range(3):
        for j in range(3):
            for k in range(3):
                offset = i * 9 + j * 3 + k
                window = padded[:, i : i + extent[0], j : j + extent[1], k : k + extent[2]]
                summed = summed + jnp.sum(blocks[offset].astype(jnp.float32) * window[None], axis=1)
    return summed


def node_strain(padded):
    extent = (padded.shape[1] - 2, padded.shape[2] - 2, padded.shape[3] - 2)

    def gradient(c, k):
        lower = [slice(1, 1 + extent[0]), slice(1, 1 + extent[1]), slice(1, 1 + extent[2])]
        upper = list(lower)
        lower[k] = slice(0, extent[k])
        upper[k] = slice(2, 2 + extent[k])
        return (padded[c][tuple(upper)] - padded[c][tuple(lower)]) * 0.5

    table = [[gradient(c, k) for k in range(3)] for c in range(3)]
    return jnp.stack(
        [
            table[0][0],
            table[1][1],
            table[2][2],
            table[1][2] + table[2][1],
            table[0][2] + table[2][0],
            table[0][1] + table[1][0],
        ]
    )


def activity(branch):
    bit_index = jnp.arange(SLIP, dtype=jnp.int32)
    return (jnp.right_shift(branch[None], bit_index[:, None, None, None]) & 1).astype(jnp.float32)


def elastic_matrix(diagonal, offdiag):
    return (
        offdiag.reshape((6, 6) + offdiag.shape[1:])
        + jnp.eye(6, dtype=jnp.float32)[:, :, None, None, None] * diagonal[None]
    )


def make_entry(diagonal, offdiag, schmid_rows, critical, plastic_rate):
    matrix = elastic_matrix(diagonal, offdiag)
    schmid_mat = schmid_rows.reshape((12, 6) + schmid_rows.shape[1:])
    return (
        matrix,
        schmid_mat,
        critical[:, None],
        plastic_rate[:, None],
        jnp.swapaxes(schmid_mat, 0, 1),
    )


def contract(matrix, field):
    summed = matrix[:, 0][:, None] * field[0][None]
    for j in range(1, matrix.shape[1]):
        summed = summed + matrix[:, j][:, None] * field[j][None]
    return summed


def sweeps(ebar, entry, plane_sum):
    baseline = ebar[:, :, None, None, None]
    matrix, schmid_mat, critical, plastic_rate, schmid_back = entry
    shape = (6, ebar.shape[1]) + matrix.shape[2:]
    fluctuation = jnp.zeros(shape, jnp.float32)
    plastic = jnp.zeros(shape, jnp.float32)
    for sweep in range(SWEEPS):
        strain = baseline + fluctuation - plastic
        stress = contract(matrix, strain)
        resolved = contract(schmid_mat, stress)
        slipped = plastic_rate * (resolved - critical * jnp.tanh(resolved / critical))
        plastic = plastic + contract(schmid_back, slipped)
        beside = (
            plane_sum(strain, stress) + jnp.roll(stress, 1, axis=3) + jnp.roll(stress, -1, axis=3)
        )
        beside = beside + jnp.roll(stress, 1, axis=4) + jnp.roll(stress, -1, axis=4)
        fluctuation = fluctuation - RELAX * (stress - NEIGHBOUR_WEIGHT * beside)
    final_strain = baseline + fluctuation - plastic
    return contract(matrix, final_strain)


def ring_place(index):
    high, low = index // 4, index % 4
    return 4 * high + 2 * ((low // 2 + high) % 2) + low % 2


def volume_kernel(
    members,
    groups,
    displacement,
    stiffness,
    external,
    node,
    owner,
    load,
    diag,
    off,
    schmid,
    crss,
    branch,
    rate,
    residual,
    point_stress,
    diag_v,
    off_v,
    schmid_v,
    crss_v,
    branch_v,
    rate_v,
    strain_v,
    stress_v,
    edge_v,
    halo_v,
    stiff_v,
    extended_v,
    shifted_v,
    own_part,
    all_parts,
    own_total,
    all_totals,
    own_sum,
    all_sums,
    own_back,
    all_back,
    send_sems,
    recv_sems,
    local_sems,
    edge_send,
    edge_recv,
    layer_send,
    layer_recv,
    member_send,
    member_recv,
    group_send,
    group_recv,
):
    points = groups
    parts = 6 * points
    listed = node.shape[0]
    me, mine = lax.axis_index("rve"), lax.axis_index("grp")
    linear, devices = mine * members + me, groups * members
    place = ring_place(me)
    sources = [off, diag, schmid, crss, branch, rate]
    targets = [off_v, diag_v, schmid_v, crss_v, branch_v, rate_v]

    def slab_part(number):
        number = number % devices
        return {"grp": number // members, "rve": number % members}

    barrier = pltpu.get_barrier_semaphore()
    greeted = [{"rve": (me + k) % members} for k in range(1, members)]
    greeted += [{"grp": (mine + k) % groups} for k in range(1, groups)]
    greeted += [slab_part(linear + 1), slab_part(linear + devices - 1)]
    for device in greeted:
        pl.semaphore_signal(barrier, inc=1, device_id=device, device_id_type=MESH)
    pl.semaphore_wait(barrier, len(greeted))

    layers = []
    for way in range(2):
        layers.append(
            pltpu.make_async_remote_copy(
                src_ref=displacement.at[:, 1 - way],
                dst_ref=extended_v.at[:, 3 * way],
                send_sem=layer_send.at[way],
                recv_sem=layer_recv.at[way],
                device_id=slab_part(linear + (1 if way == 0 else devices - 1)),
                device_id_type=MESH,
            )
        )
        layers[way].start()
    stiff_copy = pltpu.make_async_copy(stiffness, stiff_v, local_sems.at[6])
    stiff_copy.start()

    def block_of(source, device):
        rows = pl.ds(pl.multiple_of(ring_place(device) * 8, 8), 8)
        return source.at[0, :, 0, rows, :]

    def start_blocks(which):
        copies = []
        for n in which:
            for k in range(1, members):
                peer = (me + k) % members
                copies.append(
                    pltpu.make_async_remote_copy(
                        src_ref=block_of(sources[n], peer),
                        dst_ref=targets[n].at[me],
                        send_sem=send_sems.at[n, k],
                        recv_sem=recv_sems.at[n, k],
                        device_id={"rve": peer},
                        device_id_type=MESH,
                    )
                )
                copies[-1].start()
            copies.append(
                pltpu.make_async_copy(
                    block_of(sources[n], me), targets[n].at[me], local_sems.at[n]
                )
            )
            copies[-1].start()
        return copies

    def to_members(stage, source, target):
        target[me] = source[...]
        copies = []
        for k in range(1, members):
            copies.append(
                pltpu.make_async_remote_copy(
                    src_ref=source,
                    dst_ref=target.at[me],
                    send_sem=member_send.at[stage, k],
                    recv_sem=member_recv.at[stage, k],
                    device_id={"rve": (me + k) % members},
                    device_id_type=MESH,
                )
            )
            copies[-1].start()
        return copies

    def to_groups(stage, source, target):
        target[mine] = source[mine]
        copies = []
        for k in range(1, groups):
            peer = (mine + k) % groups
            copies.append(
                pltpu.make_async_remote_copy(
                    src_ref=source.at[peer],
                    dst_ref=target.at[mine],
                    send_sem=group_send.at[stage, k],
                    recv_sem=group_recv.at[stage, k],
                    device_id={"grp": peer},
                    device_id_type=MESH,
                )
            )
            copies[-1].start()
        return copies

    def member_totals(gathered, target):
        for g in range(groups):
            total = gathered[0, g]
            for r in range(1, members):
                total = total + gathered[r, g]
            target[g] = jnp.broadcast_to(jnp.sum(total, axis=1, keepdims=True), (8, 128))

    elastic_blocks = start_blocks([0, 1])

    ny, nz = displacement.shape[2:]
    for d in range(3):
        for x in range(2):
            extended_v[d, x + 1] = displacement[d, x]
    for copy in layers:
        copy.wait()
    for d in range(3):
        extended_v[d, 0] = jnp.where(linear == 0, 0.0, extended_v[d, 0])
        extended_v[d, 3] = jnp.where(linear == devices - 1, 0.0, extended_v[d, 3])
    node_row = lax.broadcasted_iota(jnp.int32, (ny, nz), 0)
    node_lane = lax.broadcasted_iota(jnp.int32, (ny, nz), 1)
    position = node_row * nz + node_lane

    def shift(n, carry):
        d, x = n // 4, n % 4
        value = extended_v[d, x]
        for j in range(3):
            line = value
            if j == 0:
                line = jnp.where(node_row == 0, 0.0, pltpu.roll(value, 1, 0))
            if j == 2:
                line = jnp.where(node_row == ny - 1, 0.0, pltpu.roll(value, ny - 1, 0))
            shifted_v[3 * j, d, x] = jnp.where(node_lane == 0, 0.0, pltpu.roll(line, 1, 1))
            shifted_v[3 * j + 1, d, x] = line
            shifted_v[3 * j + 2, d, x] = jnp.where(
                node_lane == nz - 1, 0.0, pltpu.roll(line, nz - 1, 1)
            )
        return carry

    lax.fori_loop(0, 12, shift, 0)

    def gradient(c, k, x):
        if k == 0:
            return (extended_v[c, x + 2] - extended_v[c, x]) * 0.5
        low, high = ((1, 7), (3, 5))[k - 1]
        return (shifted_v[high, c, x + 1] - shifted_v[low, c, x + 1]) * 0.5

    starts = [node[p] - me * (2 * ny * nz) for p in range(listed)]
    found = [[None] * 6 for p in range(listed)]
    for i, terms in enumerate(
        [[(0, 0)], [(1, 1)], [(2, 2)], [(1, 2), (2, 1)], [(0, 2), (2, 0)], [(0, 1), (1, 0)]]
    ):
        for x in range(2):
            value = gradient(*terms[0], x)
            for term in terms[1:]:
                value = value + gradient(*term, x)
            for p in range(listed):
                picked = jnp.where(position == starts[p] - x * (ny * nz), value, 0.0)
                found[p][i] = picked if x == 0 else found[p][i] + picked
    own_part[...] = jnp.zeros_like(own_part)
    for i in range(6):
        lines = [jnp.sum(found[p][i], axis=0, keepdims=True) for p in range(listed)]
        for g in range(groups):
            line = jnp.where(owner[0, 0] == g, lines[0], 0.0)
            for p in range(1, listed):
                line = line + jnp.where(owner[p, 0] == g, lines[p], 0.0)
            own_part[g, i : i + 1, :] = line
    strain_parts = to_members(0, own_part, all_parts)
    slip_blocks = start_blocks([2, 3, 4, 5])

    stiff_copy.wait()

    def couple(o, sums):
        i, w = o // 9, o % 9
        out = list(sums)
        for x in range(2):
            window = [shifted_v[w, d, x + i] for d in range(3)]
            for c in range(3):
                for d in range(3):
                    block = stiff_v[o, c, d, x].astype(jnp.float32)
                    out[3 * x + c] = out[3 * x + c] + block * window[d]
        return tuple(out)

    zero = jnp.zeros((ny, nz), jnp.float32)
    applied = lax.fori_loop(0, 27, couple, (zero,) * 6)
    for x in range(2):
        for c in range(3):
            residual[c, x] = external[c, x] - applied[3 * x + c]

    for copy in strain_parts:
        copy.wait()
    member_totals(all_parts, own_total)
    for copy in to_groups(0, own_total, all_totals):
        copy.wait()
    for copy in elastic_blocks:
        copy.wait()

    def elastic(v, strain):
        stress = []
        for i in range(6):
            sums = [None] * points
            for j in range(6):
                c = off_v[v, 6 * i + j]
                for p in range(points):
                    term = c * strain[6 * p + j]
                    sums[p] = term if j == 0 else sums[p] + term
            stress.append(sums)
        return [stress[i][p] for p in range(points) for i in range(6)]

    def keep(v, now, stress):
        for k in range(parts):
            stress_v[now, v, k] = stress[k]
            edge_v[now, 0, v, k : k + 1, :] = stress[k][7:8, :]
            edge_v[now, 1, v, k : k + 1, :] = stress[k][0:1, :]

    following = ring_place((place + 1) % members)
    previous = ring_place((place + members - 1) % members)

    def edge_copies(now, chunk):
        planes = pl.ds(chunk * CHUNK, CHUNK)
        return [
            pltpu.make_async_remote_copy(
                src_ref=edge_v.at[now, way, planes],
                dst_ref=halo_v.at[now, way, planes],
                send_sem=edge_send.at[now, way, chunk],
                recv_sem=edge_recv.at[now, way, chunk],
                device_id={"rve": following if way == 0 else previous},
                device_id_type=MESH,
            )
            for way in range(2)
        ]

    def begin(chunk, carry):
        for n in range(CHUNK):
            v = chunk * CHUNK + n
            for i in range(6):
                off_v[v, 7 * i] = off_v[v, 7 * i] + diag_v[v, i]
            strain = []
            for p in range(points):
                for i in range(6):
                    value = jnp.broadcast_to(all_totals[p, i : i + 1, :], (8, 128))
                    strain_v[v, 6 * p + i] = value
                    strain.append(value)
            keep(v, 0, elastic(v, strain))
        for copy in edge_copies(0, chunk):
            copy.start()
        return carry

    lax.fori_loop(0, members // CHUNK, begin, 0)
    for copy in slip_blocks:
        copy.wait()

    def prepare(v, carry):
        bits, speed = branch_v[v, 0], rate_v[v, 0]
        for a in range(SLIP):
            critical = crss_v[v, a]
            inverse = 1.0 / critical
            for i in range(6):
                schmid_v[v, 6 * a + i] = schmid_v[v, 6 * a + i] * inverse
            active = ((bits >> a) & 1).astype(jnp.float32)
            crss_v[v, a] = active * speed * (critical * critical)
        return carry

    lax.fori_loop(0, members, prepare, 0)
    row = lax.broadcasted_iota(jnp.int32, (8, 128), 0)
    top, bottom = row == 0, row == 7

    def slip(now, v):
        for half in range(0, points, 2):
            pair = range(half, min(half + 2, points))
            stress = {(p, i): stress_v[now, v, 6 * p + i] for p in pair for i in range(6)}
            change = {}
            for a in range(SLIP):
                rows = [schmid_v[v, 6 * a + i] for i in range(6)]
                weight = crss_v[v, a]
                for p in pair:
                    ratio = rows[0] * stress[p, 0]
                    for i in range(1, 6):
                        ratio = ratio + rows[i] * stress[p, i]
                    slipped = weight * (ratio - jnp.tanh(ratio))
                    for i in range(6):
                        term = rows[i] * slipped
                        change[p, i] = term if a == 0 else change[p, i] + term
            for p in pair:
                for i in range(6):
                    strain_v[v, 6 * p + i] = strain_v[v, 6 * p + i] - change[p, i]

    def advance(now, v):
        before, after = (v + members - 1) % members, (v + 1) % members
        strain = []
        for k in range(parts):
            stress = stress_v[now, v, k]
            above = jnp.where(top, halo_v[now, 0, v, k : k + 1, :], pltpu.roll(stress, 1, 0))
            below = jnp.where(bottom, halo_v[now, 1, v, k : k + 1, :], pltpu.roll(stress, 7, 0))
            beside = (stress_v[now, before, k] + stress_v[now, after, k]) + (above + below)
            beside = beside + (pltpu.roll(stress, 1, 1) + pltpu.roll(stress, 127, 1))
            value = strain_v[v, k] - RELAX * (stress - NEIGHBOUR_WEIGHT * beside)
            strain_v[v, k] = value
            strain.append(value)
        keep(v, 1 - now, elastic(v, strain))

    def sweep(s, carry):
        now = s % 2

        def slip_plane(v, inner):
            slip(now, v)
            return inner

        def advance_planes(chunk, inner):
            for copy in edge_copies(now, chunk):
                copy.wait()
            for n in range(CHUNK):
                advance(now, chunk * CHUNK + n)

            @pl.when(s < SWEEPS - 1)
            def _():
                for copy in edge_copies(1 - now, chunk):
                    copy.start()

            return inner

        lax.fori_loop(0, members, slip_plane, 0)
        lax.fori_loop(0, members // CHUNK, advance_planes, 0)
        return carry

    lax.fori_loop(0, SWEEPS, sweep, 0)
    last = SWEEPS % 2
    own_sum[...] = jnp.zeros_like(own_sum)
    for p in range(points):
        for i in range(6):
            total = stress_v[last, 0, 6 * p + i]
            for v in range(1, members):
                total = total + stress_v[last, v, 6 * p + i]
            own_sum[p, i : i + 1, :] = jnp.sum(total, axis=0, keepdims=True)
    for copy in to_members(1, own_sum, all_sums):
        copy.wait()
    member_totals(all_sums, own_back)
    for copy in to_groups(1, own_back, all_back):
        copy.wait()
    voxels = members * 8 * members * 128
    for p in range(listed):
        value = jnp.where(owner[p, 0] == 0, all_back[0], 0.0)
        for g in range(1, groups):
            value = value + jnp.where(owner[p, 0] == g, all_back[g], 0.0)
        value = value / voxels
        point_stress[p] = value
        for c in range(3):
            force = load[p, 6 * c] * value[0:1, :]
            for j in range(1, 6):
                force = force + load[p, 6 * c + j] * value[j : j + 1, :]
            for x in range(2):
                here = position == starts[p] - x * (ny * nz)
                residual[c, x] = residual[c, x] - jnp.where(here, force, 0.0)


def in_one_kernel(mesh_sizes, displacement, stiffness, external, node, owner, load, *volume):
    groups, members = mesh_sizes
    parts = 6 * groups
    any_space = pl.BlockSpec(memory_space=pl.ANY)
    vector = pl.BlockSpec(memory_space=pltpu.VMEM)
    scalar = pl.BlockSpec(memory_space=pltpu.SMEM)

    def held(count, dtype=jnp.float32):
        return pltpu.VMEM((members, count, 8, 128), dtype)

    def sems(*shape):
        return pltpu.SemaphoreType.DMA(shape)

    extent = displacement.shape[2:]
    small = pltpu.VMEM((groups, 8, 128), jnp.float32)
    gathered = pltpu.VMEM((members, groups, 8, 128), jnp.float32)
    edges = pltpu.VMEM((2, 2, members, parts, 128), jnp.float32)
    chunks = members // CHUNK
    diag, off, schmid, crss, branch, rate = volume
    residual, stress = pl.pallas_call(
        functools.partial(volume_kernel, members, groups),
        out_shape=(
            jax.ShapeDtypeStruct(external.shape, jnp.float32),
            jax.ShapeDtypeStruct((node.shape[0], 8, 128), jnp.float32),
        ),
        in_specs=[vector, any_space, vector] + [scalar] * 3 + [any_space] * 6,
        out_specs=(vector, vector),
        scratch_shapes=[
            held(6),
            held(36),
            held(72),
            held(12),
            held(1, jnp.int32),
            held(1),
            held(parts),
            pltpu.VMEM((2, members, parts, 8, 128), jnp.float32),
            edges,
            edges,
            pltpu.VMEM(stiffness.shape, stiffness.dtype),
            pltpu.VMEM((3, 4) + extent, jnp.float32),
            pltpu.VMEM((9, 3, 4) + extent, jnp.float32),
            small,
            gathered,
            small,
            small,
            small,
            gathered,
            small,
            small,
            sems(6, members),
            sems(6, members),
            sems(7),
            sems(2, 2, chunks),
            sems(2, 2, chunks),
            sems(2),
            sems(2),
            sems(2, members),
            sems(2, members),
            sems(2, groups),
            sems(2, groups),
        ],
        compiler_params=pltpu.CompilerParams(
            collective_id=0, has_side_effects=True, vmem_limit_bytes=48 * 1024 * 1024
        ),
        cost_estimate=pl.CostEstimate(
            flops=20 * 180 * parts * members * 1024, bytes_accessed=8 << 20, transcendentals=0
        ),
    )(
        displacement, stiffness, external, node, owner, load, diag, off, schmid, crss,
        branch[None], rate[None],
    )
    return residual, stress[:, :6, 0]


def plane_sums(ebar, moduli_diag, moduli_off, schmid, crss, branch, rate):
    plastic_rate = activity(branch[0]) * rate[0]
    entry = make_entry(moduli_diag[0], moduli_off[0], schmid[0], crss[0], plastic_rate)

    def plane_sum(strain, stress):
        rimmed = padded_2(stress, (("rve", 2),), 1, True)
        return rimmed[:, :, :-2] + rimmed[:, :, 2:]

    final = sweeps(ebar, entry, plane_sum)
    return jnp.sum(final, axis=(2, 3, 4))


def per_device(
    displacement,
    stiffness,
    external,
    point_node,
    point_owner,
    point_load,
    moduli_diag,
    moduli_off,
    schmid,
    crss,
    branch,
    rate,
):
    sizes = (lax.axis_size("grp"), lax.axis_size("rve"))
    fits = sizes[1] == 8 and rate.shape[1:] == (1, 64, 128) and displacement.shape[1] == 2
    if fits and point_node.shape[0] == 2:
        return in_one_kernel(
            sizes, displacement, stiffness, external, point_node, point_owner, point_load,
            moduli_diag, moduli_off, schmid, crss, branch, rate,
        )
    extended = padded_2(displacement, ((("grp", "rve"), 1),), 1, False)
    padded = jnp.pad(extended, ((0, 0), (0, 0), (1, 1), (1, 1)))
    applied = stiff_apply(stiffness, padded)
    strain_field = node_strain(padded).reshape(6, -1)
    groups = lax.axis_size("grp")
    members = lax.axis_size("rve")
    member = lax.axis_index("rve")
    local_nodes = strain_field.shape[1]
    shifted_node = point_node - member * local_nodes
    present = ((shifted_node >= 0) & (shifted_node < local_nodes)).astype(jnp.float32)
    safe_node = jnp.clip(shifted_node, 0, local_nodes - 1)
    partial_value = strain_field[:, safe_node].T * present[:, None]
    count = point_owner.shape[0]
    capacity = count // 2
    owner = point_owner[:, 0]
    onehot = (owner[:, None] == jnp.arange(groups, dtype=jnp.int32)[None, :]).astype(jnp.float32)
    ranked = jnp.cumsum(onehot, axis=0) - onehot
    slot_of = jnp.sum(ranked * onehot, axis=1)
    slot_match = (
        slot_of[None, None, :] == jnp.arange(capacity, dtype=jnp.float32)[None, :, None]
    ).astype(jnp.float32)
    select = onehot.T[:, None, :] * slot_match
    quarter = lax.psum(partial_value, "rve")
    outgoing = jnp.einsum("gsp,pi->gsi", select, quarter, precision=lax.Precision.HIGHEST)
    arrived = lax.all_to_all(outgoing, "grp", split_axis=0, concat_axis=0, tiled=True)
    ebar = arrived.reshape(-1, 6).T
    voxels = members * rate.shape[1] * rate.shape[2] * rate.shape[3]
    local_sums = plane_sums(ebar, moduli_diag, moduli_off, schmid, crss, branch, rate)
    totals = lax.psum(local_sums, "rve") / voxels
    returned = lax.all_to_all(
        jnp.transpose(totals.reshape(6, groups, capacity), (1, 2, 0)),
        "grp",
        split_axis=0,
        concat_axis=0,
        tiled=True,
    )
    point_stress = jnp.einsum("gsp,gsi->pi", select, returned, precision=lax.Precision.HIGHEST)
    force = jnp.einsum(
        "pcj,pj->pc", point_load.reshape(-1, 3, 6), point_stress, precision=lax.Precision.HIGHEST
    )
    flat = (external - applied).reshape(3, -1).at[:, safe_node].add(-(force * present[:, None]).T)
    return (flat.reshape(external.shape), point_stress)


def solution(mesh):
    in_specs = (
        P(None, ("grp", "rve"), None, None),
        P(None, None, None, ("grp", "rve"), None, None),
        P(None, ("grp", "rve"), None, None),
        P("grp"),
        P("grp", None),
        P("grp", None),
        P("grp", None, "rve", None, None),
        P("grp", None, "rve", None, None),
        P("grp", None, "rve", None, None),
        P("grp", None, "rve", None, None),
        P("grp", "rve", None, None),
        P("grp", "rve", None, None),
    )
    out_specs = (P(None, ("grp", "rve"), None, None), P("grp", None))
    return jax.shard_map(
        per_device, mesh=mesh, in_specs=in_specs, out_specs=out_specs, check_vma=False
    )
```

```python
import functools
import jax
import jax.numpy as jnp
from jax import lax
from jax.experimental import pallas as pl
from jax.experimental.pallas import tpu as pltpu
from jax.sharding import PartitionSpec as P

MESH = pl.DeviceIdType.MESH
CHUNK = 2
PIECES = 4

SLIP = 12
SWEEPS = 10


RELAX = 0.15
NEIGHBOUR_WEIGHT = 1.0 / 6.0


def padded_2(value, sides, width, wrap):
    for axis, dim in sides:
        count, length = (lax.axis_size(axis), value.shape[dim])
        up = [(i, (i + 1) % count) for i in range(count if wrap else count - 1)]
        down = [(j, i) for i, j in up]
        last = lax.slice_in_dim(value, length - width, length, axis=dim)
        first = lax.slice_in_dim(value, 0, width, axis=dim)
        before = lax.ppermute(last, axis, up)
        after = lax.ppermute(first, axis, down)
        value = jnp.concatenate([before, value, after], axis=dim)
    return value


def stiff_apply(blocks, padded):
    extent = (padded.shape[1] - 2, padded.shape[2] - 2, padded.shape[3] - 2)
    summed = jnp.zeros((3,) + extent, jnp.float32)
    for i in range(3):
        for j in range(3):
            for k in range(3):
                offset = i * 9 + j * 3 + k
                window = padded[:, i : i + extent[0], j : j + extent[1], k : k + extent[2]]
                summed = summed + jnp.sum(blocks[offset].astype(jnp.float32) * window[None], axis=1)
    return summed


def node_strain(padded):
    extent = (padded.shape[1] - 2, padded.shape[2] - 2, padded.shape[3] - 2)

    def gradient(c, k):
        lower = [slice(1, 1 + extent[0]), slice(1, 1 + extent[1]), slice(1, 1 + extent[2])]
        upper = list(lower)
        lower[k] = slice(0, extent[k])
        upper[k] = slice(2, 2 + extent[k])
        return (padded[c][tuple(upper)] - padded[c][tuple(lower)]) * 0.5

    table = [[gradient(c, k) for k in range(3)] for c in range(3)]
    return jnp.stack(
        [
            table[0][0],
            table[1][1],
            table[2][2],
            table[1][2] + table[2][1],
            table[0][2] + table[2][0],
            table[0][1] + table[1][0],
        ]
    )


def activity(branch):
    bit_index = jnp.arange(SLIP, dtype=jnp.int32)
    return (jnp.right_shift(branch[None], bit_index[:, None, None, None]) & 1).astype(jnp.float32)


def elastic_matrix(diagonal, offdiag):
    return (
        offdiag.reshape((6, 6) + offdiag.shape[1:])
        + jnp.eye(6, dtype=jnp.float32)[:, :, None, None, None] * diagonal[None]
    )


def make_entry(diagonal, offdiag, schmid_rows, critical, plastic_rate):
    matrix = elastic_matrix(diagonal, offdiag)
    schmid_mat = schmid_rows.reshape((12, 6) + schmid_rows.shape[1:])
    return (
        matrix,
        schmid_mat,
        critical[:, None],
        plastic_rate[:, None],
        jnp.swapaxes(schmid_mat, 0, 1),
    )


def contract(matrix, field):
    summed = matrix[:, 0][:, None] * field[0][None]
    for j in range(1, matrix.shape[1]):
        summed = summed + matrix[:, j][:, None] * field[j][None]
    return summed


def sweeps(ebar, entry, plane_sum):
    baseline = ebar[:, :, None, None, None]
    matrix, schmid_mat, critical, plastic_rate, schmid_back = entry
    shape = (6, ebar.shape[1]) + matrix.shape[2:]
    fluctuation = jnp.zeros(shape, jnp.float32)
    plastic = jnp.zeros(shape, jnp.float32)
    for sweep in range(SWEEPS):
        strain = baseline + fluctuation - plastic
        stress = contract(matrix, strain)
        resolved = contract(schmid_mat, stress)
        slipped = plastic_rate * (resolved - critical * jnp.tanh(resolved / critical))
        plastic = plastic + contract(schmid_back, slipped)
        beside = (
            plane_sum(strain, stress) + jnp.roll(stress, 1, axis=3) + jnp.roll(stress, -1, axis=3)
        )
        beside = beside + jnp.roll(stress, 1, axis=4) + jnp.roll(stress, -1, axis=4)
        fluctuation = fluctuation - RELAX * (stress - NEIGHBOUR_WEIGHT * beside)
    final_strain = baseline + fluctuation - plastic
    return contract(matrix, final_strain)


def ring_place(index):
    high, low = index // 4, index % 4
    return 4 * high + 2 * ((low // 2 + high) % 2) + low % 2


def volume_kernel(
    members,
    groups,
    displacement,
    stiffness,
    external,
    node,
    owner,
    load,
    diag,
    off,
    schmid,
    crss,
    branch,
    rate,
    residual,
    point_stress,
    own_diag,
    own_off,
    external_v,
    off_v,
    schmid_v,
    crss_v,
    branch_v,
    rate_v,
    strain_v,
    stress_v,
    edge_v,
    halo_v,
    stiff_v,
    extended_v,
    shifted_v,
    own_part,
    all_parts,
    own_total,
    all_totals,
    own_sum,
    all_sums,
    own_back,
    all_back,
    send_sems,
    recv_sems,
    local_sems,
    edge_send,
    edge_recv,
    layer_send,
    layer_recv,
    member_send,
    member_recv,
    group_send,
    group_recv,
):
    points = groups
    parts = 6 * points
    listed = node.shape[0]
    me, mine = lax.axis_index("rve"), lax.axis_index("grp")
    linear, devices = mine * members + me, groups * members
    place = ring_place(me)

    def slab_part(number):
        number = number % devices
        return {"grp": number // members, "rve": number % members}

    barrier = pltpu.get_barrier_semaphore()
    greeted = [{"rve": (me + k) % members} for k in range(1, members)]
    greeted += [{"grp": (mine + k) % groups} for k in range(1, groups)]
    greeted += [slab_part(linear + 1), slab_part(linear + devices - 1)]
    for device in greeted:
        pl.semaphore_signal(barrier, inc=1, device_id=device, device_id_type=MESH)
    pl.semaphore_wait(barrier, len(greeted))

    near = [
        pltpu.make_async_copy(off.at[0, :, 0], own_off, local_sems.at[0]),
        pltpu.make_async_copy(diag.at[0, :, 0], own_diag, local_sems.at[1]),
        pltpu.make_async_copy(displacement, extended_v.at[:, 1:3], local_sems.at[2]),
        pltpu.make_async_copy(external, external_v, local_sems.at[3]),
        pltpu.make_async_copy(stiffness, stiff_v, local_sems.at[4]),
    ]
    layers = []
    for way in range(2):
        layers.append(
            pltpu.make_async_remote_copy(
                src_ref=displacement.at[:, 1 - way],
                dst_ref=extended_v.at[:, 3 * way],
                send_sem=layer_send.at[way],
                recv_sem=layer_recv.at[way],
                device_id=slab_part(linear + (1 if way == 0 else devices - 1)),
                device_id_type=MESH,
            )
        )
        layers[way].start()
    for copy in near:
        copy.start()

    def start_blocks(number, source, target):
        copies = []

        def block_of(device):
            rows = pl.ds(pl.multiple_of(ring_place(device) * 8, 8), 8)
            return source.at[:, rows, :]

        for k in range(1, members):
            peer = (me + k) % members
            copies.append(
                pltpu.make_async_remote_copy(
                    src_ref=block_of(peer),
                    dst_ref=target.at[me],
                    send_sem=send_sems.at[number, k],
                    recv_sem=recv_sems.at[number, k],
                    device_id={"rve": peer},
                    device_id_type=MESH,
                )
            )
            copies[-1].start()
        copies.append(
            pltpu.make_async_copy(block_of(me), target.at[me], local_sems.at[5 + number])
        )
        copies[-1].start()
        return copies

    def to_members(stage, source, target):
        target[me] = source[...]
        copies = []
        for k in range(1, members):
            copies.append(
                pltpu.make_async_remote_copy(
                    src_ref=source,
                    dst_ref=target.at[me],
                    send_sem=member_send.at[stage, k],
                    recv_sem=member_recv.at[stage, k],
                    device_id={"rve": (me + k) % members},
                    device_id_type=MESH,
                )
            )
            copies[-1].start()
        return copies

    def to_groups(stage, source, target):
        target[mine] = source[mine]
        copies = []
        for k in range(1, groups):
            peer = (mine + k) % groups
            copies.append(
                pltpu.make_async_remote_copy(
                    src_ref=source.at[peer],
                    dst_ref=target.at[mine],
                    send_sem=group_send.at[stage, k],
                    recv_sem=group_recv.at[stage, k],
                    device_id={"grp": peer},
                    device_id_type=MESH,
                )
            )
            copies[-1].start()
        return copies

    def member_totals(gathered, target):
        for g in range(groups):
            total = gathered[0, g]
            for r in range(1, members):
                total = total + gathered[r, g]
            target[g] = jnp.broadcast_to(jnp.sum(total, axis=1, keepdims=True), (8, 128))

    weight_blocks = start_blocks(0, crss.at[0, :, 0], crss_v)
    weight_blocks += start_blocks(1, branch.at[0, :, 0], branch_v)
    weight_blocks += start_blocks(2, rate.at[0, :, 0], rate_v)
    near[0].wait()
    near[1].wait()
    for i in range(6):
        own_off[7 * i] = own_off[7 * i] + own_diag[i]
    elastic_blocks = start_blocks(3, own_off, off_v)

    ny, nz = displacement.shape[2:]
    near[2].wait()
    for copy in layers:
        copy.wait()
    for d in range(3):
        extended_v[d, 0] = jnp.where(linear == 0, 0.0, extended_v[d, 0])
        extended_v[d, 3] = jnp.where(linear == devices - 1, 0.0, extended_v[d, 3])
    node_row = lax.broadcasted_iota(jnp.int32, (ny, nz), 0)
    node_lane = lax.broadcasted_iota(jnp.int32, (ny, nz), 1)
    position = node_row * nz + node_lane

    def shift(n, carry):
        d, x = n // 4, n % 4
        value = extended_v[d, x]
        for j in range(3):
            line = value
            if j == 0:
                line = jnp.where(node_row == 0, 0.0, pltpu.roll(value, 1, 0))
            if j == 2:
                line = jnp.where(node_row == ny - 1, 0.0, pltpu.roll(value, ny - 1, 0))
            shifted_v[3 * j, d, x] = jnp.where(node_lane == 0, 0.0, pltpu.roll(line, 1, 1))
            shifted_v[3 * j + 1, d, x] = line
            shifted_v[3 * j + 2, d, x] = jnp.where(
                node_lane == nz - 1, 0.0, pltpu.roll(line, nz - 1, 1)
            )
        return carry

    lax.fori_loop(0, 12, shift, 0)

    def gradient(c, k, x):
        if k == 0:
            return (extended_v[c, x + 2] - extended_v[c, x]) * 0.5
        low, high = ((1, 7), (3, 5))[k - 1]
        return (shifted_v[high, c, x + 1] - shifted_v[low, c, x + 1]) * 0.5

    starts = [node[p] - me * (2 * ny * nz) for p in range(listed)]
    found = [[None] * 6 for p in range(listed)]
    for i, terms in enumerate(
        [[(0, 0)], [(1, 1)], [(2, 2)], [(1, 2), (2, 1)], [(0, 2), (2, 0)], [(0, 1), (1, 0)]]
    ):
        for x in range(2):
            value = gradient(*terms[0], x)
            for term in terms[1:]:
                value = value + gradient(*term, x)
            for p in range(listed):
                picked = jnp.where(position == starts[p] - x * (ny * nz), value, 0.0)
                found[p][i] = picked if x == 0 else found[p][i] + picked
    own_part[...] = jnp.zeros_like(own_part)
    for i in range(6):
        lines = [jnp.sum(found[p][i], axis=0, keepdims=True) for p in range(listed)]
        for g in range(groups):
            line = jnp.where(owner[0, 0] == g, lines[0], 0.0)
            for p in range(1, listed):
                line = line + jnp.where(owner[p, 0] == g, lines[p], 0.0)
            own_part[g, i : i + 1, :] = line
    strain_parts = to_members(0, own_part, all_parts)
    systems = SLIP // PIECES
    slip_blocks = []
    for n in range(PIECES):
        which = pl.ds(6 * systems * n, 6 * systems)
        slip_blocks.append(
            start_blocks(4 + n, schmid.at[0, which, 0], schmid_v.at[:, which])
        )

    near[3].wait()
    near[4].wait()

    def couple(o, sums):
        i, w = o // 9, o % 9
        out = list(sums)
        for x in range(2):
            window = [shifted_v[w, d, x + i] for d in range(3)]
            for c in range(3):
                for d in range(3):
                    block = stiff_v[o, c, d, x].astype(jnp.float32)
                    out[3 * x + c] = out[3 * x + c] + block * window[d]
        return tuple(out)

    zero = jnp.zeros((ny, nz), jnp.float32)
    applied = lax.fori_loop(0, 27, couple, (zero,) * 6)
    for x in range(2):
        for c in range(3):
            residual[c, x] = external_v[c, x] - applied[3 * x + c]

    for copy in strain_parts:
        copy.wait()
    member_totals(all_parts, own_total)
    for copy in to_groups(0, own_total, all_totals):
        copy.wait()
    for copy in elastic_blocks:
        copy.wait()

    def elastic(v, strain):
        stress = []
        for i in range(6):
            sums = [None] * points
            for j in range(6):
                c = off_v[v, 6 * i + j]
                for p in range(points):
                    term = c * strain[6 * p + j]
                    sums[p] = term if j == 0 else sums[p] + term
            stress.append(sums)
        return [stress[i][p] for p in range(points) for i in range(6)]

    def keep(v, now, stress):
        for k in range(parts):
            stress_v[now, v, k] = stress[k]
            edge_v[now, 0, v, k : k + 1, :] = stress[k][7:8, :]
            edge_v[now, 1, v, k : k + 1, :] = stress[k][0:1, :]

    following = ring_place((place + 1) % members)
    previous = ring_place((place + members - 1) % members)

    def edge_copies(now, chunk):
        planes = pl.ds(chunk * CHUNK, CHUNK)
        return [
            pltpu.make_async_remote_copy(
                src_ref=edge_v.at[now, way, planes],
                dst_ref=halo_v.at[now, way, planes],
                send_sem=edge_send.at[now, way, chunk],
                recv_sem=edge_recv.at[now, way, chunk],
                device_id={"rve": following if way == 0 else previous},
                device_id_type=MESH,
            )
            for way in range(2)
        ]

    def begin(chunk, carry):
        for n in range(CHUNK):
            v = chunk * CHUNK + n
            strain = []
            for p in range(points):
                for i in range(6):
                    value = jnp.broadcast_to(all_totals[p, i : i + 1, :], (8, 128))
                    strain_v[v, 6 * p + i] = value
                    strain.append(value)
            keep(v, 0, elastic(v, strain))
        for copy in edge_copies(0, chunk):
            copy.start()
        return carry

    lax.fori_loop(0, members // CHUNK, begin, 0)
    for copy in weight_blocks:
        copy.wait()

    def prepare(v, part):
        bits, speed = branch_v[v, 0], rate_v[v, 0]
        for a in part:
            critical = crss_v[v, a]
            inverse = 1.0 / critical
            for i in range(6):
                schmid_v[v, 6 * a + i] = schmid_v[v, 6 * a + i] * inverse
            active = ((bits >> a) & 1).astype(jnp.float32)
            crss_v[v, a] = active * speed * (critical * critical)

    row = lax.broadcasted_iota(jnp.int32, (8, 128), 0)
    top, bottom = row == 0, row == 7

    def slip(now, v, part):
        for half in range(0, points, 2):
            pair = range(half, min(half + 2, points))
            stress = {(p, i): stress_v[now, v, 6 * p + i] for p in pair for i in range(6)}
            change = {}
            for a in part:
                rows = [schmid_v[v, 6 * a + i] for i in range(6)]
                weight = crss_v[v, a]
                for p in pair:
                    ratio = rows[0] * stress[p, 0]
                    for i in range(1, 6):
                        ratio = ratio + rows[i] * stress[p, i]
                    slipped = weight * (ratio - jnp.tanh(ratio))
                    for i in range(6):
                        term = rows[i] * slipped
                        change[p, i] = term if a == part[0] else change[p, i] + term
            for p in pair:
                for i in range(6):
                    strain_v[v, 6 * p + i] = strain_v[v, 6 * p + i] - change[p, i]

    def advance(now, v):
        before, after = (v + members - 1) % members, (v + 1) % members
        strain = []
        for k in range(parts):
            stress = stress_v[now, v, k]
            above = jnp.where(top, halo_v[now, 0, v, k : k + 1, :], pltpu.roll(stress, 1, 0))
            below = jnp.where(bottom, halo_v[now, 1, v, k : k + 1, :], pltpu.roll(stress, 7, 0))
            beside = (stress_v[now, before, k] + stress_v[now, after, k]) + (above + below)
            beside = beside + (pltpu.roll(stress, 1, 1) + pltpu.roll(stress, 127, 1))
            value = strain_v[v, k] - RELAX * (stress - NEIGHBOUR_WEIGHT * beside)
            strain_v[v, k] = value
            strain.append(value)
        keep(v, 1 - now, elastic(v, strain))

    def advance_all(s):
        now = s % 2

        def advance_planes(chunk, inner):
            for copy in edge_copies(now, chunk):
                copy.wait()
            for n in range(CHUNK):
                advance(now, chunk * CHUNK + n)

            @pl.when(s < SWEEPS - 1)
            def _():
                for copy in edge_copies(1 - now, chunk):
                    copy.start()

            return inner

        lax.fori_loop(0, members // CHUNK, advance_planes, 0)

    def sweep(s, carry):
        def slip_plane(v, inner):
            slip(s % 2, v, range(SLIP))
            return inner

        @pl.when(s > 0)
        def _():
            lax.fori_loop(0, members, slip_plane, 0)

        advance_all(s)
        return carry

    for n in range(PIECES):
        for copy in slip_blocks[n]:
            copy.wait()
        part = range(systems * n, systems * (n + 1))

        def slip_piece(v, carry, part=part):
            prepare(v, part)
            slip(0, v, part)
            return carry

        lax.fori_loop(0, members, slip_piece, 0)
    lax.fori_loop(0, SWEEPS, sweep, 0)
    last = SWEEPS % 2
    own_sum[...] = jnp.zeros_like(own_sum)
    for p in range(points):
        for i in range(6):
            total = stress_v[last, 0, 6 * p + i]
            for v in range(1, members):
                total = total + stress_v[last, v, 6 * p + i]
            own_sum[p, i : i + 1, :] = jnp.sum(total, axis=0, keepdims=True)
    for copy in to_members(1, own_sum, all_sums):
        copy.wait()
    member_totals(all_sums, own_back)
    for copy in to_groups(1, own_back, all_back):
        copy.wait()
    voxels = members * 8 * members * 128
    for p in range(listed):
        value = jnp.where(owner[p, 0] == 0, all_back[0], 0.0)
        for g in range(1, groups):
            value = value + jnp.where(owner[p, 0] == g, all_back[g], 0.0)
        value = value / voxels
        point_stress[p] = value
        for c in range(3):
            force = load[p, 6 * c] * value[0:1, :]
            for j in range(1, 6):
                force = force + load[p, 6 * c + j] * value[j : j + 1, :]
            for x in range(2):
                here = position == starts[p] - x * (ny * nz)
                residual[c, x] = residual[c, x] - jnp.where(here, force, 0.0)


def in_one_kernel(mesh_sizes, displacement, stiffness, external, node, owner, load, *volume):
    groups, members = mesh_sizes
    parts = 6 * groups
    far = pl.BlockSpec(memory_space=pltpu.HBM)
    vector = pl.BlockSpec(memory_space=pltpu.VMEM)
    scalar = pl.BlockSpec(memory_space=pltpu.SMEM)

    def held(count, dtype=jnp.float32):
        return pltpu.VMEM((members, count, 8, 128), dtype)

    def sems(*shape):
        return pltpu.SemaphoreType.DMA(shape)

    extent = displacement.shape[2:]
    small = pltpu.VMEM((groups, 8, 128), jnp.float32)
    gathered = pltpu.VMEM((members, groups, 8, 128), jnp.float32)
    edges = pltpu.VMEM((2, 2, members, parts, 128), jnp.float32)
    chunks = members // CHUNK
    diag, off, schmid, crss, branch, rate = volume
    residual, stress = pl.pallas_call(
        functools.partial(volume_kernel, members, groups),
        out_shape=(
            jax.ShapeDtypeStruct(external.shape, jnp.float32),
            jax.ShapeDtypeStruct((node.shape[0], 8, 128), jnp.float32),
        ),
        in_specs=[far] * 3 + [scalar] * 3 + [far] * 6,
        out_specs=(vector, vector),
        scratch_shapes=[
            pltpu.VMEM((6,) + rate.shape[2:], jnp.float32),
            pltpu.VMEM((36,) + rate.shape[2:], jnp.float32),
            pltpu.VMEM(external.shape, jnp.float32),
            held(36),
            held(72),
            held(12),
            held(1, jnp.int32),
            held(1),
            held(parts),
            pltpu.VMEM((2, members, parts, 8, 128), jnp.float32),
            edges,
            edges,
            pltpu.VMEM(stiffness.shape, stiffness.dtype),
            pltpu.VMEM((3, 4) + extent, jnp.float32),
            pltpu.VMEM((9, 3, 4) + extent, jnp.float32),
            small,
            gathered,
            small,
            small,
            small,
            gathered,
            small,
            small,
            sems(4 + PIECES, members),
            sems(4 + PIECES, members),
            sems(9 + PIECES),
            sems(2, 2, chunks),
            sems(2, 2, chunks),
            sems(2),
            sems(2),
            sems(2, members),
            sems(2, members),
            sems(2, groups),
            sems(2, groups),
        ],
        compiler_params=pltpu.CompilerParams(
            collective_id=0, has_side_effects=True, vmem_limit_bytes=56 * 1024 * 1024
        ),
        cost_estimate=pl.CostEstimate(
            flops=20 * 180 * parts * members * 1024, bytes_accessed=8 << 20, transcendentals=0
        ),
    )(
        displacement, stiffness, external, node, owner, load, diag, off, schmid, crss,
        branch[None], rate[None],
    )
    return residual, stress[:, :6, 0]


def plane_sums(ebar, moduli_diag, moduli_off, schmid, crss, branch, rate):
    plastic_rate = activity(branch[0]) * rate[0]
    entry = make_entry(moduli_diag[0], moduli_off[0], schmid[0], crss[0], plastic_rate)

    def plane_sum(strain, stress):
        rimmed = padded_2(stress, (("rve", 2),), 1, True)
        return rimmed[:, :, :-2] + rimmed[:, :, 2:]

    final = sweeps(ebar, entry, plane_sum)
    return jnp.sum(final, axis=(2, 3, 4))


def per_device(
    displacement,
    stiffness,
    external,
    point_node,
    point_owner,
    point_load,
    moduli_diag,
    moduli_off,
    schmid,
    crss,
    branch,
    rate,
):
    sizes = (lax.axis_size("grp"), lax.axis_size("rve"))
    fits = sizes[1] == 8 and rate.shape[1:] == (1, 64, 128) and displacement.shape[1] == 2
    if fits and point_node.shape[0] == 2:
        return in_one_kernel(
            sizes, displacement, stiffness, external, point_node, point_owner, point_load,
            moduli_diag, moduli_off, schmid, crss, branch, rate,
        )
    extended = padded_2(displacement, ((("grp", "rve"), 1),), 1, False)
    padded = jnp.pad(extended, ((0, 0), (0, 0), (1, 1), (1, 1)))
    applied = stiff_apply(stiffness, padded)
    strain_field = node_strain(padded).reshape(6, -1)
    groups = lax.axis_size("grp")
    members = lax.axis_size("rve")
    member = lax.axis_index("rve")
    local_nodes = strain_field.shape[1]
    shifted_node = point_node - member * local_nodes
    present = ((shifted_node >= 0) & (shifted_node < local_nodes)).astype(jnp.float32)
    safe_node = jnp.clip(shifted_node, 0, local_nodes - 1)
    partial_value = strain_field[:, safe_node].T * present[:, None]
    count = point_owner.shape[0]
    capacity = count // 2
    owner = point_owner[:, 0]
    onehot = (owner[:, None] == jnp.arange(groups, dtype=jnp.int32)[None, :]).astype(jnp.float32)
    ranked = jnp.cumsum(onehot, axis=0) - onehot
    slot_of = jnp.sum(ranked * onehot, axis=1)
    slot_match = (
        slot_of[None, None, :] == jnp.arange(capacity, dtype=jnp.float32)[None, :, None]
    ).astype(jnp.float32)
    select = onehot.T[:, None, :] * slot_match
    quarter = lax.psum(partial_value, "rve")
    outgoing = jnp.einsum("gsp,pi->gsi", select, quarter, precision=lax.Precision.HIGHEST)
    arrived = lax.all_to_all(outgoing, "grp", split_axis=0, concat_axis=0, tiled=True)
    ebar = arrived.reshape(-1, 6).T
    voxels = members * rate.shape[1] * rate.shape[2] * rate.shape[3]
    local_sums = plane_sums(ebar, moduli_diag, moduli_off, schmid, crss, branch, rate)
    totals = lax.psum(local_sums, "rve") / voxels
    returned = lax.all_to_all(
        jnp.transpose(totals.reshape(6, groups, capacity), (1, 2, 0)),
        "grp",
        split_axis=0,
        concat_axis=0,
        tiled=True,
    )
    point_stress = jnp.einsum("gsp,gsi->pi", select, returned, precision=lax.Precision.HIGHEST)
    force = jnp.einsum(
        "pcj,pj->pc", point_load.reshape(-1, 3, 6), point_stress, precision=lax.Precision.HIGHEST
    )
    flat = (external - applied).reshape(3, -1).at[:, safe_node].add(-(force * present[:, None]).T)
    return (flat.reshape(external.shape), point_stress)


def solution(mesh):
    in_specs = (
        P(None, ("grp", "rve"), None, None),
        P(None, None, None, ("grp", "rve"), None, None),
        P(None, ("grp", "rve"), None, None),
        P("grp"),
        P("grp", None),
        P("grp", None),
        P("grp", None, "rve", None, None),
        P("grp", None, "rve", None, None),
        P("grp", None, "rve", None, None),
        P("grp", None, "rve", None, None),
        P("grp", "rve", None, None),
        P("grp", "rve", None, None),
    )
    out_specs = (P(None, ("grp", "rve"), None, None), P("grp", None))
    return jax.shard_map(
        per_device, mesh=mesh, in_specs=in_specs, out_specs=out_specs, check_vma=False
    )
```
